32 devices in a mesh: vx: 8 (over z, x), vy: 4 (over y, core).
Axes of the slice: x: 2, y: 2, z: 4, core: 2. Of those that a mesh axis runs over, the one named last changes fastest.
Arguments:
- fields: bfloat16 [4, 512, 640, 128], P(None, 'vx', 'vy'), may hold values from -6 to 6
- modulus: bfloat16 [512, 640, 128], P('vx', 'vy'), as said below
- anchors: int32 [8, 4, 14, 3], P('vx', 'vy'), may hold values from 0 to 10, as said below
- home_count: int32 [8, 4], P('vx', 'vy'), may hold values from 1 to 14, as said below
Outputs:
- gradient: float32 [512, 640, 128], P('vx', 'vy')
The draws below stay inside these ranges and needn't reach their ends.
Inputs may be any that keep to these rules, and one draw needn't show every extreme that they name: `anchors`: column 0 is at most 4, column 1 at most 10, column 2 at most 2. `home_count`: the counts of the 8 tiles that share a vy index sum to 56. The modulus's real parts are positive and at least three times its imaginary parts, which are positive.
All inputs are finite; a program needn't handle non-finite values.
Results may differ from the reference program's by a relative error of at most 0.0003.
Values may be sent and summed in bfloat16 or wider, within the bound.
A program may use at most 192 MiB of HBM per device.

```python
import jax
import jax.numpy as jnp
from jax import lax

NF = 4
SUB = 32
HALO = 16
TX = 64
TY = 160
NZ = 64
HOME = 14
WORK = 7
RFWD = 3
NX = 512
NY = 640
N_VX = 8
N_VY = 4


def draw_modulus(key, part):
    first, second = jax.random.split(jax.random.fold_in(key, 11))
    real = jax.random.uniform(first, (NX, NY, NZ), jnp.float32, 0.5, 1.5)
    imag = real * jax.random.uniform(second, (NX, NY, NZ), jnp.float32, 0.1, 0.33)
    return jnp.concatenate([real, imag], axis=-1).astype(jnp.bfloat16)


def draw_anchors(key, part):
    keys = jax.random.split(jax.random.fold_in(key, 23), 3)
    across = jax.random.randint(keys[0], (N_VX, N_VY, HOME), 0, TX // HALO + 1)
    along = jax.random.randint(keys[1], (N_VX, N_VY, HOME), 0, TY // HALO + 1)
    depth = jax.random.randint(keys[2], (N_VX, N_VY, HOME), 0, NZ // HALO - 1)
    across = across.at[:, :, 0].set(TX // HALO)
    along = along.at[:, :, 0].set(TY // HALO)
    return jnp.stack([across, along, depth], axis=-1).astype(jnp.int32)


def draw_home_count(key, part):
    first, second = jax.random.split(jax.random.fold_in(key, 37))
    others = N_VX - 1
    rest = N_VX * WORK - HOME
    base = rest // others
    extra = rest % others
    values = jnp.concatenate([jnp.full((1,), HOME, jnp.int32), base + (jnp.arange(others) < extra).astype(jnp.int32)])
    values = jnp.broadcast_to(values[:, None], (N_VX, N_VY))
    pairs = others // 2
    shifts = jax.random.randint(first, (pairs, N_VY), 0, base)
    values = values.at[1:1 + 2 * pairs:2].add(-shifts)
    values = values.at[2:2 + 2 * pairs:2].add(shifts)
    scores = jax.random.randint(second, (N_VX, N_VY), 0, 2 ** 20) * N_VX + jnp.arange(N_VX, dtype=jnp.int32)[:, None]
    order = jnp.argsort(scores, axis=0)
    return jnp.take_along_axis(values, order, axis=0).astype(jnp.int32)


def levels(rng, extent, shards, least, top_value):
    def one(position, blocks):
        draws = jax.random.uniform(jax.random.fold_in(jax.random.fold_in(rng, 6), position), (blocks,), jnp.float32, least / len(shards), top_value / len(shards))
        return jnp.repeat(jnp.exp(draws), extent[position] // blocks).reshape((-1,) + (1,) * (len(extent) - position - 1))

    loudness = one(*shards[0])
    for cut in shards[1:]:
        loudness = loudness * one(*cut)
    return loudness


def normal_values(key, dims, deviation, reach, cuts=(), kind=jnp.bfloat16):
    entries = jax.random.normal(key, dims, jnp.float32) * deviation
    if len(cuts) > 0:
        entries = levels(key, dims, cuts, -0.22, 0.18) * entries
    return jnp.clip(entries, min=-reach, max=reach).astype(kind)


def setup_inputs(seed: int = 0) -> dict:
    seeds = jax.random.split(jax.random.key(seed), 5)
    return {
        "fields": normal_values(seeds[0], (NF, NX, NY, 2 * NZ), 1.0, 6.0, ((1, 8), (2, 4))),
        "modulus": draw_modulus(jax.random.fold_in(seeds[4], 71), 0),
        "anchors": draw_anchors(jax.random.fold_in(seeds[4], 71), 0),
        "home_count": draw_home_count(jax.random.fold_in(seeds[4], 71), 0),
    }


OMEGA = 0.07

def laplace(field):
    padded = jnp.pad(field, ((0, 0), (1, 1), (1, 1), (0, 0), (1, 1)))
    beside = padded[:, 2:, 1:-1, :, 1:-1] + padded[:, :-2, 1:-1, :, 1:-1]
    beside = beside + padded[:, 1:-1, 2:, :, 1:-1] + padded[:, 1:-1, :-2, :, 1:-1]
    beside = beside + padded[:, 1:-1, 1:-1, :, 2:] + padded[:, 1:-1, 1:-1, :, :-2]
    return 6.0 * field - beside

def cmul(left, right):
    real = left[..., 0, :] * right[..., 0, :] - left[..., 1, :] * right[..., 1, :]
    imag = left[..., 0, :] * right[..., 1, :] + left[..., 1, :] * right[..., 0, :]
    return jnp.stack([real, imag], axis=-2)

def conjugate(value):
    return jnp.stack([value[..., 0, :], -value[..., 1, :]], axis=-2)

def subzone_grad(block):
    measured = block[:-1]
    stiff = block[-1:]
    stiff_conj = conjugate(stiff)
    forward = jnp.zeros_like(measured)
    images = []
    for sweep in range(RFWD):
        image = laplace(forward)
        images.append(image)
        forward = forward + OMEGA * (measured - forward - cmul(stiff, image))
    adjoint = forward - measured
    result = jnp.zeros_like(measured[0])
    for sweep in range(RFWD - 1, 0, -1):
        result = result - OMEGA * lax.optimization_barrier(jnp.sum(cmul(adjoint, conjugate(images[sweep])), axis=0))
        if sweep > 1:
            adjoint = adjoint - OMEGA * (adjoint + laplace(cmul(stiff_conj, adjoint)))
    return result

def reference(fields, modulus, anchors, home_count):
    data = jnp.concatenate([fields, modulus[None]], axis=0)
    data = jnp.pad(data, ((0, 0), (HALO, HALO), (HALO, HALO), (0, 0)))
    data = data.reshape(NF + 1, NX + 2 * HALO, NY + 2 * HALO, 2, NZ)
    slots = jnp.arange(HOME, dtype=jnp.int32)
    live = slots[None, None, :] < home_count[:, :, None]
    rows = jnp.arange(N_VX, dtype=jnp.int32)[:, None, None] * TX + HALO * anchors[..., 0]
    cols = jnp.arange(N_VY, dtype=jnp.int32)[None, :, None] * TY + HALO * anchors[..., 1]
    depth = HALO * anchors[..., 2]
    corners = jnp.stack([rows, cols, depth], axis=-1).reshape(-1, 3).astype(jnp.int32)
    order = jnp.argsort(jnp.where(live.reshape(-1), 0, 1).astype(jnp.int32), stable=True)
    corners = corners[order[:N_VX * N_VY * WORK]]
    zero = jnp.zeros((), jnp.int32)

    def one(corner):
        block = lax.dynamic_slice(data, (zero, corner[0], corner[1], zero, corner[2]), (NF + 1, SUB, SUB, 2, SUB))
        return subzone_grad(block.astype(jnp.float32))
    grads = lax.map(one, corners, batch_size=32)
    total = jnp.zeros((NX + 2 * HALO, NY + 2 * HALO, 2, NZ), jnp.float32)

    def deposit(index, total):
        corner = corners[index]
        start = (corner[0], corner[1], zero, corner[2])
        current = lax.dynamic_slice(total, start, (SUB, SUB, 2, SUB))
        return lax.dynamic_update_slice(total, current + grads[index], start)
    total = lax.fori_loop(0, N_VX * N_VY * WORK, deposit, total)
    return total[HALO:HALO + NX, HALO:HALO + NY].reshape(NX, NY, 2 * NZ)
```

```python
import functools

import jax
import jax.numpy as jnp
import numpy as np
from jax import lax
from jax.experimental import pallas as pl
from jax.experimental.pallas import tpu as pltpu
from jax.sharding import PartitionSpec as P

NF = 4
SUB = 32
HALO = 16
OMEGA = 0.07
LANES = 128
NZ = 64
PLANES = 4
A_PLANES = 8
FIRST = 8


def constants():
    starts = (NZ - SUB) // HALO + 1
    second = 6.0 * np.eye(SUB) - np.eye(SUB, k=1) - np.eye(SUB, k=-1)
    tri = np.kron(np.eye(NF), second)
    pick = np.zeros((starts, NF, LANES, 4, LANES))
    spread = np.zeros((starts, LANES, 2, LANES))
    gather = np.zeros((starts, 2, 2, LANES, LANES))
    for s in range(starts):
        for f in range(NF):
            for z in range(SUB):
                for part in range(2):
                    source = part * NZ + s * HALO + z
                    lane = f * SUB + z
                    pick[s, f, source, part, lane] = 1.0
                    pick[s, f, source, 2 + part] = tri[lane]
                    spread[s, source, part, lane] = 1.0
                    gather[s, part, :, lane, source] = 1.0
    bf16 = jnp.bfloat16
    return (
        jnp.asarray(pick.reshape(starts, NF * LANES, 4 * LANES), bf16),
        jnp.asarray(spread.reshape(starts, LANES, 2 * LANES), bf16),
        jnp.asarray(gather.reshape(starts, 4 * LANES, LANES), bf16),
        jnp.asarray(np.concatenate([tri, tri], axis=0), bf16),
    )


def split(value):
    high = value.astype(jnp.bfloat16)
    low = (value - high.astype(jnp.float32)).astype(jnp.bfloat16)
    return high, low


def neighbours(ref, x):
    low = ref[x, FIRST : FIRST + SUB]
    high = ref[x + 2, FIRST : FIRST + SUB]
    left = ref[x + 1, FIRST - 1 : FIRST - 1 + SUB]
    right = ref[x + 1, FIRST + 1 : FIRST + 1 + SUB]
    return (low + high) + (left + right)


def center(ref, x):
    return ref[x + 1, FIRST : FIRST + SUB]


def stencil_z(real, imag, x, tri):
    rows = PLANES * SUB
    parts = []
    for ref in (real, imag):
        value = ref[pl.ds(x + 1, PLANES), FIRST : FIRST + SUB].reshape(rows, LANES)
        parts.append(jnp.concatenate(split(value), axis=1))
    return jnp.dot(
        jnp.concatenate(parts, axis=0), tri, preferred_element_type=jnp.float32
    )


def work(group, slots, kinds, tx, ty, n_sources, *refs):
    refs = list(refs)
    take = lambda count: [refs.pop(0) for _ in range(count)]
    (info,) = take(1)
    sources = [take(2) for _ in range(n_sources)]
    (start_total,) = take(1) if group == 2 else (None,)
    pick, spread, gather, tri = take(4)
    outs = take({0: 1, 1: 1, 2: 2}[group])
    (order, fbuf, mbuf, total, ur, ui, wr, wi, qr, qi) = take(10)
    (zur, zui, l1r, l1i, v3r, v3i, gr, gi, mur, mui) = take(10)
    sems, out_sem = take(2)

    x_base = tx - HALO if group == 1 else -HALO
    blocks = (tx // HALO, ty // HALO)

    start_copy = None
    for ref in (ur, ui, wr, wi, qr, qi):
        plane = jnp.zeros((FIRST + SUB + 8, LANES), jnp.float32)
        ref[0] = plane
        ref[SUB + 1] = plane

        def edge(x, carry, ref=ref):
            row = jnp.zeros((8, LANES), jnp.float32)
            ref[x, 0:FIRST] = row
            ref[x, FIRST + SUB :] = row
            return carry

        lax.fori_loop(1, SUB + 1, edge, 0)

    def clear(x, carry):
        total[x] = jnp.zeros(total.shape[1:], jnp.float32)
        return carry

    lax.fori_loop(0, total.shape[0], clear, 0)
    if group == 2:
        start_copy = pltpu.make_async_copy(
            start_total, total.at[HALO : HALO + tx, HALO : HALO + ty], out_sem.at[0]
        )
        start_copy.start()
        start_copy.wait()

    def listed(slot, count):
        mine = info[4 * slot] == kinds

        @pl.when(mine)
        def _():
            order[count] = slot

        return count + jnp.where(mine, 1, 0)

    count = lax.fori_loop(0, slots, listed, jnp.int32(0))

    def place(item):
        slot = order[item]
        return info[4 * slot + 1], info[4 * slot + 2], info[4 * slot + 3]

    def transfers(item, slot, starting):
        bx0, by0, _ = place(item)
        for dx in range(2):
            for dy in range(2):
                bx, by = bx0 + dx, by0 + dy
                rows = pl.ds(dx * HALO, HALO)
                cols = pl.ds(dy * HALO, HALO)
                to_f = fbuf.at[slot, :, rows, cols, :]
                to_m = mbuf.at[slot, rows, cols, :]
                quarter = 2 * dx + dy
                outside = (bx < 0) | (by < 0)
                past_x = bx >= blocks[0]
                past_y = by >= blocks[1]
                conditions = [jnp.logical_not(past_x) & jnp.logical_not(past_y)]
                if n_sources > 1:
                    conditions.append(jnp.logical_not(past_x) & past_y)
                if n_sources > 2:
                    conditions.append(past_x & jnp.logical_not(past_y))
                    conditions.append(past_x & past_y)
                for kind, condition in enumerate(conditions):
                    @pl.when(jnp.logical_not(outside) & condition)
                    def _(kind=kind):
                        f_ref, m_ref = sources[kind]
                        r = 0 if kind >= 2 else pl.multiple_of(bx * HALO, HALO)
                        c = 0 if kind in (1, 3) else pl.multiple_of(by * HALO, HALO)
                        box = (pl.ds(r, HALO), pl.ds(c, HALO), slice(None))
                        for which, (a, b) in enumerate(
                            ((f_ref.at[(slice(None),) + box], to_f), (m_ref.at[box], to_m))
                        ):
                            copy = pltpu.make_async_copy(a, b, sems.at[slot, quarter, which])
                            if starting:
                                copy.start()
                            else:
                                copy.wait()
                if starting:
                    @pl.when(outside)
                    def _():
                        fbuf[slot, :, dx * HALO : dx * HALO + HALO, dy * HALO : dy * HALO + HALO, :] = jnp.zeros(
                            (NF, HALO, HALO, LANES), jnp.bfloat16
                        )
                        mbuf[slot, dx * HALO : dx * HALO + HALO, dy * HALO : dy * HALO + HALO, :] = jnp.zeros(
                            (HALO, HALO, LANES), jnp.bfloat16
                        )

    @pl.when(count > 0)
    def _():
        transfers(jnp.int32(0), 0, True)

    def subzone(item, carry):
        slot = lax.rem(item, 2)

        @pl.when(item + 1 < count)
        def _():
            transfers(item + 1, 1 - slot, True)

        transfers(item, slot, False)
        bx0, by0, depth = place(item)

        def load(step, carry):
            x = step * A_PLANES
            rows = A_PLANES * SUB
            shape = (A_PLANES, SUB, LANES)
            block = jnp.concatenate(
                [fbuf[slot, f, pl.ds(x, A_PLANES)].reshape(rows, LANES) for f in range(NF)], axis=1
            )
            got = jnp.dot(block, pick[depth], preferred_element_type=jnp.float32)
            ur[pl.ds(x + 1, A_PLANES), FIRST : FIRST + SUB] = got[:, :LANES].reshape(shape)
            ui[pl.ds(x + 1, A_PLANES), FIRST : FIRST + SUB] = got[:, LANES : 2 * LANES].reshape(shape)
            zur[pl.ds(x, A_PLANES)] = got[:, 2 * LANES : 3 * LANES].reshape(shape)
            zui[pl.ds(x, A_PLANES)] = got[:, 3 * LANES :].reshape(shape)
            stiff = mbuf[slot, pl.ds(x, A_PLANES)].reshape(rows, LANES)
            mu = jnp.dot(stiff, spread[depth], preferred_element_type=jnp.float32)
            mur[pl.ds(x, A_PLANES)] = mu[:, :LANES].reshape(shape)
            mui[pl.ds(x, A_PLANES)] = mu[:, LANES:].reshape(shape)
            return carry

        lax.fori_loop(0, SUB // A_PLANES, load, 0)

        def second(step, carry):
            for p in range(PLANES):
                x = step * PLANES + p
                ir = OMEGA * (zur[x] - neighbours(ur, x))
                ii = OMEGA * (zui[x] - neighbours(ui, x))
                l1r[x] = ir
                l1i[x] = ii
                mr, mi = mur[x], mui[x]
                keep = OMEGA * (2.0 - OMEGA)
                wr[x + 1, FIRST : FIRST + SUB] = keep * center(ur, x) - OMEGA * (mr * ir - mi * ii)
                wi[x + 1, FIRST : FIRST + SUB] = keep * center(ui, x) - OMEGA * (mr * ii + mi * ir)
            return carry

        lax.fori_loop(0, SUB // PLANES, second, 0)

        def third(step, carry):
            z = stencil_z(wr, wi, step * PLANES, tri[...])
            for p in range(PLANES):
                x = step * PLANES + p
                ir = z[p * SUB : (p + 1) * SUB] - neighbours(wr, x)
                ii = z[(PLANES + p) * SUB : (PLANES + p + 1) * SUB] - neighbours(wi, x)
                mr, mi = mur[x], mui[x]
                vr = (1.0 - OMEGA) * (center(wr, x) - center(ur, x)) - OMEGA * (mr * ir - mi * ii)
                vi = (1.0 - OMEGA) * (center(wi, x) - center(ui, x)) - OMEGA * (mr * ii + mi * ir)
                v3r[x] = vr
                v3i[x] = vi
                qr[x + 1, FIRST : FIRST + SUB] = mr * vr + mi * vi
                qi[x + 1, FIRST : FIRST + SUB] = mr * vi - mi * vr
                gr[x] = vr * ir + vi * ii
                gi[x] = vi * ir - vr * ii
            return carry

        lax.fori_loop(0, SUB // PLANES, third, 0)

        row0 = bx0 * HALO - x_base
        col0 = pl.multiple_of((by0 + 1) * HALO, HALO)

        def fourth(step, carry):
            z = stencil_z(qr, qi, step * PLANES, tri[...])
            parts = []
            for p in range(PLANES):
                x = step * PLANES + p
                jr = z[p * SUB : (p + 1) * SUB] - neighbours(qr, x)
                ji = z[(PLANES + p) * SUB : (PLANES + p + 1) * SUB] - neighbours(qi, x)
                vr = (1.0 - OMEGA) * v3r[x] - OMEGA * jr
                vi = (1.0 - OMEGA) * v3i[x] - OMEGA * ji
                ir, ii = l1r[x], l1i[x]
                sr = -OMEGA * (gr[x] + (vr * ir + vi * ii))
                si = -OMEGA * (gi[x] + (vi * ir - vr * ii))
                parts.append(jnp.concatenate(split(sr) + split(si), axis=1))
            grad = jnp.dot(
                jnp.concatenate(parts, axis=0), gather[depth], preferred_element_type=jnp.float32
            )
            for p in range(PLANES):
                x = step * PLANES + p
                total[row0 + x, pl.ds(col0, SUB)] += grad[p * SUB : (p + 1) * SUB]
            return carry

        lax.fori_loop(0, SUB // PLANES, fourth, 0)
        return carry

    lax.fori_loop(0, count, subzone, 0)

    if group == 1:
        copies = [(total.at[:, HALO : 2 * HALO + ty], outs[0])]
    else:
        copies = [(total.at[HALO : HALO + tx, HALO : HALO + ty], outs[0])]
        if group == 2:
            copies.append((total.at[HALO : HALO + tx, HALO + ty : 2 * HALO + ty], outs[1]))
    started = []
    for index, (a, b) in enumerate(copies):
        started.append(pltpu.make_async_copy(a, b, out_sem.at[1 + index]))
        started[-1].start()
    for copy in started:
        copy.wait()


def run(group, info, sources, mats, tx, ty, start=None):
    slots = info.shape[0] // 4
    f32 = jnp.float32
    total_rows = 2 * HALO if group == 1 else HALO + tx
    outs = {
        0: [(tx, ty, LANES)],
        1: [(2 * HALO, HALO + ty, LANES)],
        2: [(tx, ty, LANES), (tx, HALO, LANES)],
    }[group]
    hbm = pl.BlockSpec(memory_space=pl.ANY)
    smem = pl.BlockSpec(memory_space=pltpu.SMEM)
    vmem = pl.BlockSpec(memory_space=pltpu.VMEM)
    flat = [part for pair in sources for part in pair]
    args = [info] + flat + ([start] if start is not None else []) + list(mats)
    in_specs = [smem] + [hbm] * (len(args) - 1 - len(mats)) + [vmem] * len(mats)
    padded = pltpu.VMEM((SUB + 2, FIRST + SUB + 8, LANES), f32)
    plain = pltpu.VMEM((SUB, SUB, LANES), f32)
    return pl.pallas_call(
        functools.partial(work, group, slots, group, tx, ty, len(sources)),
        out_shape=[jax.ShapeDtypeStruct(shape, f32) for shape in outs],
        in_specs=in_specs,
        out_specs=[hbm] * len(outs),
        scratch_shapes=[
            pltpu.SMEM((slots,), jnp.int32),
            pltpu.VMEM((2, NF, SUB, SUB, LANES), jnp.bfloat16),
            pltpu.VMEM((2, SUB, SUB, LANES), jnp.bfloat16),
            pltpu.VMEM((total_rows, 2 * HALO + ty, LANES), f32),
        ]
        + [padded] * 6
        + [plain] * 10
        + [pltpu.SemaphoreType.DMA((2, 4, 2)), pltpu.SemaphoreType.DMA((3,))],
        compiler_params=pltpu.CompilerParams(vmem_limit_bytes=48 * 2**20),
        cost_estimate=pl.CostEstimate(
            flops=2 * 10**10 if group == 0 else 10**10, bytes_accessed=150 * 10**6, transcendentals=0
        ),
        name=("interior", "beyond_x", "beyond_y")[group],
    )(*args)


def shards(fields, modulus, anchors, home_count):
    tx, ty = modulus.shape[0], modulus.shape[1]
    n_x, n_y = lax.axis_size("vx"), lax.axis_size("vy")
    i, j = lax.axis_index("vx"), lax.axis_index("vy")
    both = ("vx", "vy")
    down_x = [(k + 1, k) for k in range(n_x - 1)]
    down_y = [(k + 1, k) for k in range(n_y - 1)]
    down_d = [
        ((a + 1) * n_y + b + 1, a * n_y + b) for a in range(n_x - 1) for b in range(n_y - 1)
    ]
    up_x = [(b, a) for a, b in down_x]
    up_y = [(b, a) for a, b in down_y]

    spots = anchors[0, 0]
    home = spots.shape[0]
    live = (jnp.arange(home, dtype=jnp.int32) < home_count[0, 0]).astype(jnp.int32)
    own = jnp.concatenate([spots, live[:, None]], axis=1)
    own_x = lax.ppermute(own, "vx", down_x)
    own_y = lax.ppermute(own, "vy", down_y)
    own_d = lax.ppermute(own, both, down_d)
    fx = lax.ppermute(fields[:, :HALO], "vx", down_x)
    mx = lax.ppermute(modulus[:HALO], "vx", down_x)
    fy = lax.ppermute(fields[:, :, :HALO], "vy", down_y)
    my = lax.ppermute(modulus[:, :HALO], "vy", down_y)
    fc = lax.ppermute(fields[:, :HALO, :HALO], both, down_d)
    mc = lax.ppermute(modulus[:HALO, :HALO], both, down_d)

    last_x, last_y = tx // HALO - 1, ty // HALO - 1

    def described(spot, from_x, from_y):
        o0, o1, o2, on = (spot[:, k] for k in range(4))
        ok = on > 0
        ok = ok & ((o0 == 0) if from_x else ((o0 > 0) | (i == 0)))
        ok = ok & ((o1 == 0) if from_y else ((o1 > 0) | (j == 0)))
        bx = jnp.full_like(o0, last_x) if from_x else o0 - 1
        by = jnp.full_like(o1, last_y) if from_y else o1 - 1
        kind = jnp.where(bx == last_x, 1, jnp.where(by == last_y, 2, 0))
        return jnp.stack([jnp.where(ok, kind, -1), bx, by, o2], axis=1)

    mine = described(own, False, False)
    everything = jnp.concatenate(
        [
            mine,
            described(own_x, True, False),
            described(own_y, False, True),
            described(own_d, True, True),
        ]
    )
    mats = constants()
    local = (fields, modulus)
    (inner,) = run(0, mine.reshape(-1), [local], mats, tx, ty)
    (strip,) = run(
        1, everything.reshape(-1), [local, (fy, my), (fx, mx), (fc, mc)], mats, tx, ty
    )
    from_below = lax.ppermute(strip[HALO:], "vx", up_x)
    owned, side = run(2, everything.reshape(-1), [local, (fy, my)], mats, tx, ty, inner)
    side = side.at[tx - HALO :].add(strip[:HALO, ty:])
    side = side.at[:HALO].add(from_below[:, ty:])
    from_left = lax.ppermute(side, "vy", up_y)
    owned = owned.at[tx - HALO :].add(strip[:HALO, :ty])
    owned = owned.at[:HALO].add(from_below[:, :ty])
    return owned.at[:, :HALO].add(from_left)


def solution(mesh):
    return jax.shard_map(
        shards,
        mesh=mesh,
        in_specs=(
            P(None, "vx", "vy", None),
            P("vx", "vy", None),
            P("vx", "vy", None, None),
            P("vx", "vy"),
        ),
        out_specs=P("vx", "vy", None),
        check_vma=False,
    )
```

```python
import functools

import jax
import jax.numpy as jnp
import numpy as np
from jax import lax
from jax.experimental import pallas as pl
from jax.experimental.pallas import tpu as pltpu
from jax.sharding import PartitionSpec as P

NF = 4
SUB = 32
HALO = 16
OMEGA = 0.07
LANES = 128
NZ = 64
PLANES = 8
A_PLANES = 8
FIRST = 8


def constants():
    starts = (NZ - SUB) // HALO + 1
    second = 6.0 * np.eye(SUB) - np.eye(SUB, k=1) - np.eye(SUB, k=-1)
    tri = np.kron(np.eye(NF), second)
    pick = np.zeros((starts, NF, LANES, 4, LANES))
    spread = np.zeros((starts, LANES, 2, LANES))
    gather = np.zeros((starts, 2, 2, LANES, LANES))
    for s in range(starts):
        for f in range(NF):
            for z in range(SUB):
                for part in range(2):
                    source = part * NZ + s * HALO + z
                    lane = f * SUB + z
                    pick[s, f, source, part, lane] = 1.0
                    pick[s, f, source, 2 + part] = tri[lane]
                    spread[s, source, part, lane] = 1.0
                    gather[s, part, :, lane, source] = 1.0
    bf16 = jnp.bfloat16
    return (
        jnp.asarray(pick.reshape(starts, NF * LANES, 4 * LANES), bf16),
        jnp.asarray(spread.reshape(starts, LANES, 2 * LANES), bf16),
        jnp.asarray(gather.reshape(starts, 4 * LANES, LANES), bf16),
        jnp.asarray(np.concatenate([tri, tri], axis=0), bf16),
    )


def split(value):
    high = value.astype(jnp.bfloat16)
    low = (value - high.astype(jnp.float32)).astype(jnp.bfloat16)
    return high, low


def neighbours(ref, x):
    low = ref[x, FIRST : FIRST + SUB]
    high = ref[x + 2, FIRST : FIRST + SUB]
    left = ref[x + 1, FIRST - 1 : FIRST - 1 + SUB]
    right = ref[x + 1, FIRST + 1 : FIRST + 1 + SUB]
    return (low + high) + (left + right)


def center(ref, x):
    return ref[x + 1, FIRST : FIRST + SUB]


def stencil_z(real, imag, x, tri):
    rows = PLANES * SUB
    parts = []
    for ref in (real, imag):
        value = ref[pl.ds(x + 1, PLANES), FIRST : FIRST + SUB].reshape(rows, LANES)
        parts.append(jnp.concatenate(split(value), axis=1))
    return jnp.dot(
        jnp.concatenate(parts, axis=0), tri, preferred_element_type=jnp.float32
    )


def work(group, slots, kinds, tx, ty, n_sources, *refs):
    refs = list(refs)
    take = lambda count: [refs.pop(0) for _ in range(count)]
    (info,) = take(1)
    sources = [take(2)] + [take(1) for _ in range(n_sources - 1)]
    earlier = take(group)
    pick, spread, gather, tri = take(4)
    outs = take({0: 1, 1: 1, 2: 2}[group])
    (order, buf, total, ur, ui, wr, wi, qr, qi) = take(9)
    (zur, zui, l1r, l1i, v3r, v3i, gr, gi, mur, mui) = take(10)
    sems, out_sem = take(2)
    (strip,) = take(1) if group == 2 else (None,)

    x_base = tx - HALO if group == 1 else -HALO
    blocks = (tx // HALO, ty // HALO)

    if group == 2:
        fills = [
            pltpu.make_async_copy(
                earlier[0], total.at[HALO : HALO + tx, HALO : HALO + ty], out_sem.at[0]
            ),
            pltpu.make_async_copy(earlier[1].at[:HALO], strip, out_sem.at[3]),
        ]
        for fill in fills:
            fill.start()
    for ref in (ur, ui, wr, wi, qr, qi):
        plane = jnp.zeros((FIRST + SUB + 8, LANES), jnp.float32)
        ref[0] = plane
        ref[SUB + 1] = plane

        def edge(x, carry, ref=ref):
            row = jnp.zeros((8, LANES), jnp.float32)
            ref[x, 0:FIRST] = row
            ref[x, FIRST + SUB :] = row
            return carry

        lax.fori_loop(1, SUB + 1, edge, 0)

    def clear(x, carry):
        if group == 2:
            side = jnp.zeros((HALO, LANES), jnp.float32)
            total[x, :HALO] = side
            total[x, HALO + ty :] = side
        else:
            total[x] = jnp.zeros(total.shape[1:], jnp.float32)
        return carry

    lax.fori_loop(0, total.shape[0], clear, 0)
    if group == 2:
        total[:HALO, HALO : HALO + ty] = jnp.zeros((HALO, ty, LANES), jnp.float32)

    def listed(slot, count):
        mine = info[4 * slot] == kinds

        @pl.when(mine)
        def _():
            order[count] = slot

        return count + jnp.where(mine, 1, 0)

    count = lax.fori_loop(0, slots, listed, jnp.int32(0))

    def place(item):
        slot = order[item]
        return info[4 * slot + 1], info[4 * slot + 2], info[4 * slot + 3]

    def transfers(item, slot, starting):
        bx0, by0, _ = place(item)
        for dx in range(2):
            for dy in range(2):
                bx, by = bx0 + dx, by0 + dy
                rows = pl.ds(dx * HALO, HALO)
                cols = pl.ds(dy * HALO, HALO)
                to_f = buf.at[slot, :NF, rows, cols, :]
                to_m = buf.at[slot, NF, rows, cols, :]
                to_all = buf.at[slot, :, rows, cols, :]
                quarter = 2 * dx + dy
                outside = (bx < 0) | (by < 0)
                past_x = bx >= blocks[0]
                past_y = by >= blocks[1]
                conditions = [jnp.logical_not(past_x) & jnp.logical_not(past_y)]
                if n_sources > 1:
                    conditions.append(jnp.logical_not(past_x) & past_y)
                if n_sources > 2:
                    conditions.append(past_x & jnp.logical_not(past_y))
                    conditions.append(past_x & past_y)
                for kind, condition in enumerate(conditions):
                    @pl.when(jnp.logical_not(outside) & condition)
                    def _(kind=kind):
                        r = 0 if kind >= 2 else pl.multiple_of(bx * HALO, HALO)
                        c = 0 if kind in (1, 3) else pl.multiple_of(by * HALO, HALO)
                        box = (pl.ds(r, HALO), pl.ds(c, HALO), slice(None))
                        first = sources[kind][0].at[(slice(None),) + box]
                        if kind == 0:
                            pairs = [(first, to_f), (sources[0][1].at[box], to_m)]
                        else:
                            pairs = [(first, to_all)]
                        for which, (a, b) in enumerate(pairs):
                            copy = pltpu.make_async_copy(a, b, sems.at[slot, quarter, which])
                            if starting:
                                copy.start()
                            else:
                                copy.wait()
                if starting:
                    @pl.when(outside)
                    def _():
                        buf[slot, :, dx * HALO : dx * HALO + HALO, dy * HALO : dy * HALO + HALO, :] = jnp.zeros(
                            (NF + 1, HALO, HALO, LANES), jnp.bfloat16
                        )

    @pl.when(count > 0)
    def _():
        transfers(jnp.int32(0), 0, True)

    def subzone(item, carry):
        slot = lax.rem(item, 2)

        @pl.when(item + 1 < count)
        def _():
            transfers(item + 1, 1 - slot, True)

        transfers(item, slot, False)
        bx0, by0, depth = place(item)

        def load(step, carry):
            x = step * A_PLANES
            rows = A_PLANES * SUB
            shape = (A_PLANES, SUB, LANES)
            block = jnp.concatenate(
                [buf[slot, f, pl.ds(x, A_PLANES)].reshape(rows, LANES) for f in range(NF)], axis=1
            )
            got = jnp.dot(block, pick[depth], preferred_element_type=jnp.float32)
            ur[pl.ds(x + 1, A_PLANES), FIRST : FIRST + SUB] = got[:, :LANES].reshape(shape)
            ui[pl.ds(x + 1, A_PLANES), FIRST : FIRST + SUB] = got[:, LANES : 2 * LANES].reshape(shape)
            zur[pl.ds(x, A_PLANES)] = got[:, 2 * LANES : 3 * LANES].reshape(shape)
            zui[pl.ds(x, A_PLANES)] = got[:, 3 * LANES :].reshape(shape)
            stiff = buf[slot, NF, pl.ds(x, A_PLANES)].reshape(rows, LANES)
            mu = jnp.dot(stiff, spread[depth], preferred_element_type=jnp.float32)
            mur[pl.ds(x, A_PLANES)] = mu[:, :LANES].reshape(shape)
            mui[pl.ds(x, A_PLANES)] = mu[:, LANES:].reshape(shape)
            return carry

        lax.fori_loop(0, SUB // A_PLANES, load, 0)

        def second(step, carry):
            for p in range(PLANES):
                x = step * PLANES + p
                ir = OMEGA * (zur[x] - neighbours(ur, x))
                ii = OMEGA * (zui[x] - neighbours(ui, x))
                l1r[x] = ir
                l1i[x] = ii
                mr, mi = mur[x], mui[x]
                keep = OMEGA * (2.0 - OMEGA)
                wr[x + 1, FIRST : FIRST + SUB] = keep * center(ur, x) - OMEGA * (mr * ir - mi * ii)
                wi[x + 1, FIRST : FIRST + SUB] = keep * center(ui, x) - OMEGA * (mr * ii + mi * ir)
            return carry

        lax.fori_loop(0, SUB // PLANES, second, 0)

        def third(step, carry):
            z = stencil_z(wr, wi, step * PLANES, tri[...])
            for p in range(PLANES):
                x = step * PLANES + p
                ir = z[p * SUB : (p + 1) * SUB] - neighbours(wr, x)
                ii = z[(PLANES + p) * SUB : (PLANES + p + 1) * SUB] - neighbours(wi, x)
                mr, mi = mur[x], mui[x]
                vr = (1.0 - OMEGA) * (center(wr, x) - center(ur, x)) - OMEGA * (mr * ir - mi * ii)
                vi = (1.0 - OMEGA) * (center(wi, x) - center(ui, x)) - OMEGA * (mr * ii + mi * ir)
                v3r[x] = vr
                v3i[x] = vi
                qr[x + 1, FIRST : FIRST + SUB] = mr * vr + mi * vi
                qi[x + 1, FIRST : FIRST + SUB] = mr * vi - mi * vr
                gr[x] = vr * ir + vi * ii
                gi[x] = vi * ir - vr * ii
            return carry

        lax.fori_loop(0, SUB // PLANES, third, 0)

        row0 = bx0 * HALO - x_base
        col0 = pl.multiple_of((by0 + 1) * HALO, HALO)

        def fourth(step, carry):
            z = stencil_z(qr, qi, step * PLANES, tri[...])
            parts = []
            for p in range(PLANES):
                x = step * PLANES + p
                jr = z[p * SUB : (p + 1) * SUB] - neighbours(qr, x)
                ji = z[(PLANES + p) * SUB : (PLANES + p + 1) * SUB] - neighbours(qi, x)
                vr = (1.0 - OMEGA) * v3r[x] - OMEGA * jr
                vi = (1.0 - OMEGA) * v3i[x] - OMEGA * ji
                ir, ii = l1r[x], l1i[x]
                sr = -OMEGA * (gr[x] + (vr * ir + vi * ii))
                si = -OMEGA * (gi[x] + (vi * ir - vr * ii))
                parts.append(jnp.concatenate(split(sr) + split(si), axis=1))
            grad = jnp.dot(
                jnp.concatenate(parts, axis=0), gather[depth], preferred_element_type=jnp.float32
            )
            for p in range(PLANES):
                x = step * PLANES + p
                total[row0 + x, pl.ds(col0, SUB)] += grad[p * SUB : (p + 1) * SUB]
            return carry

        lax.fori_loop(0, SUB // PLANES, fourth, 0)
        return carry

    if group == 2:
        for fill in fills:
            fill.wait()

        def joined(x, carry):
            total[tx + x, HALO:] += strip[x]
            return carry

        lax.fori_loop(0, HALO, joined, 0)

    lax.fori_loop(0, count, subzone, 0)

    if group == 1:
        copies = [(total.at[:, HALO : 2 * HALO + ty], outs[0])]
    else:
        copies = [(total.at[HALO : HALO + tx, HALO : HALO + ty], outs[0])]
        if group == 2:
            copies.append((total.at[HALO : HALO + tx, HALO + ty : 2 * HALO + ty], outs[1]))
    started = []
    for index, (a, b) in enumerate(copies):
        started.append(pltpu.make_async_copy(a, b, out_sem.at[1 + index]))
        started[-1].start()
    for copy in started:
        copy.wait()


def run(group, info, sources, mats, tx, ty, *earlier):
    slots = info.shape[0] // 4
    f32 = jnp.float32
    total_rows = 2 * HALO if group == 1 else HALO + tx
    outs = {
        0: [(tx, ty, LANES)],
        1: [(2 * HALO, HALO + ty, LANES)],
        2: [(tx, ty, LANES), (tx, HALO, LANES)],
    }[group]
    hbm = pl.BlockSpec(memory_space=pl.ANY)
    smem = pl.BlockSpec(memory_space=pltpu.SMEM)
    vmem = pl.BlockSpec(memory_space=pltpu.VMEM)
    flat = [part for pair in sources for part in pair]
    args = [info] + flat + list(earlier) + list(mats)
    in_specs = [smem] + [hbm] * (len(args) - 1 - len(mats)) + [vmem] * len(mats)
    padded = pltpu.VMEM((SUB + 2, FIRST + SUB + 8, LANES), f32)
    plain = pltpu.VMEM((SUB, SUB, LANES), f32)
    return pl.pallas_call(
        functools.partial(work, group, slots, group, tx, ty, len(sources)),
        out_shape=[jax.ShapeDtypeStruct(shape, f32) for shape in outs],
        in_specs=in_specs,
        out_specs=[hbm] * len(outs),
        scratch_shapes=[
            pltpu.SMEM((slots,), jnp.int32),
            pltpu.VMEM((2, NF + 1, SUB, SUB, LANES), jnp.bfloat16),
            pltpu.VMEM((total_rows, 2 * HALO + ty, LANES), f32),
        ]
        + [padded] * 6
        + [plain] * 10
        + [pltpu.SemaphoreType.DMA((2, 4, 2)), pltpu.SemaphoreType.DMA((4,))]
        + ([pltpu.VMEM((HALO, HALO + ty, LANES), f32)] if group == 2 else []),
        compiler_params=pltpu.CompilerParams(vmem_limit_bytes=48 * 2**20),
        cost_estimate=pl.CostEstimate(
            flops=2 * 10**10 if group == 0 else 10**10, bytes_accessed=150 * 10**6, transcendentals=0
        ),
        name=("interior", "beyond_x", "beyond_y")[group],
    )(*args)


def shards(fields, modulus, anchors, home_count):
    tx, ty = modulus.shape[0], modulus.shape[1]
    n_x, n_y = lax.axis_size("vx"), lax.axis_size("vy")
    i, j = lax.axis_index("vx"), lax.axis_index("vy")
    both = ("vx", "vy")
    down_x = [(k + 1, k) for k in range(n_x - 1)]
    down_y = [(k + 1, k) for k in range(n_y - 1)]
    down_d = [
        ((a + 1) * n_y + b + 1, a * n_y + b) for a in range(n_x - 1) for b in range(n_y - 1)
    ]
    up_x = [(b, a) for a, b in down_x]
    up_y = [(b, a) for a, b in down_y]

    spots = anchors[0, 0]
    home = spots.shape[0]
    live = (jnp.arange(home, dtype=jnp.int32) < home_count[0, 0]).astype(jnp.int32)
    own = jnp.concatenate([spots, live[:, None]], axis=1)
    own_x = lax.ppermute(own, "vx", down_x)
    own_y = lax.ppermute(own, "vy", down_y)
    own_d = lax.ppermute(own, both, down_d)
    def together(rows, cols):
        return jnp.concatenate([fields[:, rows, cols], modulus[None, rows, cols]], axis=0)

    low, full = slice(0, HALO), slice(None)
    beyond_x = lax.ppermute(together(low, full), "vx", down_x)
    corner = lax.ppermute(together(low, low), both, down_d)
    beyond_y = lax.ppermute(together(full, low), "vy", down_y)

    last_x, last_y = tx // HALO - 1, ty // HALO - 1

    def described(spot, from_x, from_y):
        o0, o1, o2, on = (spot[:, k] for k in range(4))
        ok = on > 0
        ok = ok & ((o0 == 0) if from_x else ((o0 > 0) | (i == 0)))
        ok = ok & ((o1 == 0) if from_y else ((o1 > 0) | (j == 0)))
        bx = jnp.full_like(o0, last_x) if from_x else o0 - 1
        by = jnp.full_like(o1, last_y) if from_y else o1 - 1
        kind = jnp.where(bx == last_x, 1, jnp.where(by == last_y, 2, 0))
        return jnp.stack([jnp.where(ok, kind, -1), bx, by, o2], axis=1)

    mine = described(own, False, False)
    everything = jnp.concatenate(
        [
            mine,
            described(own_x, True, False),
            described(own_y, False, True),
            described(own_d, True, True),
        ]
    )
    mats = constants()
    local = (fields, modulus)
    (inner,) = run(0, mine.reshape(-1), [local], mats, tx, ty)
    sources = [local, (beyond_y,), (beyond_x,), (corner,)]
    (strip,) = run(1, everything.reshape(-1), sources, mats, tx, ty, inner)
    from_below = lax.ppermute(strip[HALO:], "vx", up_x)
    owned, side = run(2, everything.reshape(-1), sources[:2], mats, tx, ty, inner, strip)
    side = side.at[:HALO].add(from_below[:, ty:])
    from_left = lax.ppermute(side, "vy", up_y)
    owned = owned.at[:HALO].add(from_below[:, :ty])
    return owned.at[:, :HALO].add(from_left)


def solution(mesh):
    return jax.shard_map(
        shards,
        mesh=mesh,
        in_specs=(
            P(None, "vx", "vy", None),
            P("vx", "vy", None),
            P("vx", "vy", None, None),
            P("vx", "vy"),
        ),
        out_specs=P("vx", "vy", None),
        check_vma=False,
    )
```

```python
import functools

import jax
import jax.numpy as jnp
import numpy as np
from jax import lax
from jax.experimental import pallas as pl
from jax.experimental.pallas import tpu as pltpu
from jax.sharding import PartitionSpec as P

NF = 4
SUB = 32
HALO = 16
OMEGA = 0.07
LANES = 128
NZ = 64
PLANES = 16
A_PLANES = 16
FIRST = 8


def constants():
    starts = (NZ - SUB) // HALO + 1
    second = 6.0 * np.eye(SUB) - np.eye(SUB, k=1) - np.eye(SUB, k=-1)
    tri = np.kron(np.eye(NF), second)
    pick = np.zeros((starts, NF, LANES, 4, LANES))
    spread = np.zeros((starts, LANES, 2, LANES))
    gather = np.zeros((starts, 2, 2, LANES, LANES))
    for s in range(starts):
        for f in range(NF):
            for z in range(SUB):
                for part in range(2):
                    source = part * NZ + s * HALO + z
                    lane = f * SUB + z
                    pick[s, f, source, part, lane] = 1.0
                    pick[s, f, source, 2 + part] = tri[lane]
                    spread[s, source, part, lane] = 1.0
                    gather[s, part, :, lane, source] = 1.0
    bf16 = jnp.bfloat16
    return (
        jnp.asarray(pick.reshape(starts, NF * LANES, 4 * LANES), bf16),
        jnp.asarray(spread.reshape(starts, LANES, 2 * LANES), bf16),
        jnp.asarray(gather.reshape(starts, 4 * LANES, LANES), bf16),
        jnp.asarray(np.concatenate([tri, tri], axis=0), bf16),
    )


def split(value):
    high = value.astype(jnp.bfloat16)
    low = (value - high.astype(jnp.float32)).astype(jnp.bfloat16)
    return high, low


def neighbours(ref, x):
    low = ref[x, FIRST : FIRST + SUB]
    high = ref[x + 2, FIRST : FIRST + SUB]
    left = ref[x + 1, FIRST - 1 : FIRST - 1 + SUB]
    right = ref[x + 1, FIRST + 1 : FIRST + 1 + SUB]
    return (low + high) + (left + right)


def center(ref, x):
    return ref[x + 1, FIRST : FIRST + SUB]


def stencil_z(real, imag, x, tri):
    rows = PLANES * SUB
    parts = []
    for ref in (real, imag):
        value = ref[pl.ds(x + 1, PLANES), FIRST : FIRST + SUB].reshape(rows, LANES)
        parts.append(jnp.concatenate(split(value), axis=1))
    return jnp.dot(
        jnp.concatenate(parts, axis=0), tri, preferred_element_type=jnp.float32
    )


def work(group, slots, kinds, tx, ty, n_sources, *refs):
    refs = list(refs)
    take = lambda count: [refs.pop(0) for _ in range(count)]
    (info,) = take(1)
    sources = [take(2)] + [take(1) for _ in range(n_sources - 1)]
    earlier = take(group)
    pick, spread, gather, tri = take(4)
    outs = take({0: 1, 1: 1, 2: 2}[group])
    (order, buf, total, ur, ui, wr, wi, qr, qi) = take(9)
    (zur, zui, l1r, l1i, v3r, v3i, gr, gi, mur, mui) = take(10)
    sems, out_sem = take(2)
    (strip,) = take(1) if group == 2 else (None,)

    x_base = tx - HALO if group == 1 else -HALO
    blocks = (tx // HALO, ty // HALO)

    if group == 2:
        fills = [
            pltpu.make_async_copy(
                earlier[0], total.at[HALO : HALO + tx, HALO : HALO + ty], out_sem.at[0]
            ),
            pltpu.make_async_copy(earlier[1].at[:HALO], strip, out_sem.at[3]),
        ]
        for fill in fills:
            fill.start()
    for ref in (ur, ui, wr, wi, qr, qi):
        plane = jnp.zeros((FIRST + SUB + 8, LANES), jnp.float32)
        ref[0] = plane
        ref[SUB + 1] = plane

        def edge(x, carry, ref=ref):
            row = jnp.zeros((8, LANES), jnp.float32)
            ref[x, 0:FIRST] = row
            ref[x, FIRST + SUB :] = row
            return carry

        lax.fori_loop(1, SUB + 1, edge, 0)

    def clear(x, carry):
        if group == 2:
            side = jnp.zeros((HALO, LANES), jnp.float32)
            total[x, :HALO] = side
            total[x, HALO + ty :] = side
        else:
            total[x] = jnp.zeros(total.shape[1:], jnp.float32)
        return carry

    lax.fori_loop(0, total.shape[0], clear, 0)
    if group == 2:
        total[:HALO, HALO : HALO + ty] = jnp.zeros((HALO, ty, LANES), jnp.float32)

    def listed(slot, count):
        mine = info[4 * slot] == kinds

        @pl.when(mine)
        def _():
            order[count] = slot

        return count + jnp.where(mine, 1, 0)

    count = lax.fori_loop(0, slots, listed, jnp.int32(0))

    def place(item):
        slot = order[item]
        return info[4 * slot + 1], info[4 * slot + 2], info[4 * slot + 3]

    def transfers(item, slot, starting):
        bx0, by0, _ = place(item)
        for dx in range(2):
            for dy in range(2):
                bx, by = bx0 + dx, by0 + dy
                rows = pl.ds(dx * HALO, HALO)
                cols = pl.ds(dy * HALO, HALO)
                to_f = buf.at[slot, :NF, rows, cols, :]
                to_m = buf.at[slot, NF, rows, cols, :]
                to_all = buf.at[slot, :, rows, cols, :]
                quarter = 2 * dx + dy
                outside = (bx < 0) | (by < 0)
                past_x = bx >= blocks[0]
                past_y = by >= blocks[1]
                conditions = [jnp.logical_not(past_x) & jnp.logical_not(past_y)]
                if n_sources > 1:
                    conditions.append(jnp.logical_not(past_x) & past_y)
                if n_sources > 2:
                    conditions.append(past_x & jnp.logical_not(past_y))
                    conditions.append(past_x & past_y)
                for kind, condition in enumerate(conditions):
                    @pl.when(jnp.logical_not(outside) & condition)
                    def _(kind=kind):
                        r = 0 if kind >= 2 else pl.multiple_of(bx * HALO, HALO)
                        c = 0 if kind in (1, 3) else pl.multiple_of(by * HALO, HALO)
                        box = (pl.ds(r, HALO), pl.ds(c, HALO), slice(None))
                        first = sources[kind][0].at[(slice(None),) + box]
                        if kind == 0:
                            pairs = [(first, to_f), (sources[0][1].at[box], to_m)]
                        else:
                            pairs = [(first, to_all)]
                        for which, (a, b) in enumerate(pairs):
                            copy = pltpu.make_async_copy(a, b, sems.at[slot, quarter, which])
                            if starting:
                                copy.start()
                            else:
                                copy.wait()
                if starting:
                    @pl.when(outside)
                    def _():
                        buf[slot, :, dx * HALO : dx * HALO + HALO, dy * HALO : dy * HALO + HALO, :] = jnp.zeros(
                            (NF + 1, HALO, HALO, LANES), jnp.bfloat16
                        )

    @pl.when(count > 0)
    def _():
        transfers(jnp.int32(0), 0, True)

    def subzone(item, carry):
        slot = lax.rem(item, 2)

        @pl.when(item + 1 < count)
        def _():
            transfers(item + 1, 1 - slot, True)

        transfers(item, slot, False)
        bx0, by0, depth = place(item)

        def load(step, carry):
            x = step * A_PLANES
            rows = A_PLANES * SUB
            shape = (A_PLANES, SUB, LANES)
            block = jnp.concatenate(
                [buf[slot, f, pl.ds(x, A_PLANES)].reshape(rows, LANES) for f in range(NF)], axis=1
            )
            got = jnp.dot(block, pick[depth], preferred_element_type=jnp.float32)
            ur[pl.ds(x + 1, A_PLANES), FIRST : FIRST + SUB] = got[:, :LANES].reshape(shape)
            ui[pl.ds(x + 1, A_PLANES), FIRST : FIRST + SUB] = got[:, LANES : 2 * LANES].reshape(shape)
            zur[pl.ds(x, A_PLANES)] = got[:, 2 * LANES : 3 * LANES].reshape(shape)
            zui[pl.ds(x, A_PLANES)] = got[:, 3 * LANES :].reshape(shape)
            stiff = buf[slot, NF, pl.ds(x, A_PLANES)].reshape(rows, LANES)
            mu = jnp.dot(stiff, spread[depth], preferred_element_type=jnp.float32)
            mur[pl.ds(x, A_PLANES)] = mu[:, :LANES].reshape(shape)
            mui[pl.ds(x, A_PLANES)] = mu[:, LANES:].reshape(shape)
            return carry

        lax.fori_loop(0, SUB // A_PLANES, load, 0)

        def second(step, carry):
            for p in range(PLANES):
                x = step * PLANES + p
                ir = OMEGA * (zur[x] - neighbours(ur, x))
                ii = OMEGA * (zui[x] - neighbours(ui, x))
                l1r[x] = ir
                l1i[x] = ii
                mr, mi = mur[x], mui[x]
                keep = OMEGA * (2.0 - OMEGA)
                wr[x + 1, FIRST : FIRST + SUB] = keep * center(ur, x) - OMEGA * (mr * ir - mi * ii)
                wi[x + 1, FIRST : FIRST + SUB] = keep * center(ui, x) - OMEGA * (mr * ii + mi * ir)
            return carry

        lax.fori_loop(0, SUB // PLANES, second, 0)

        def third(step, carry):
            z = stencil_z(wr, wi, step * PLANES, tri[...])
            for p in range(PLANES):
                x = step * PLANES + p
                ir = z[p * SUB : (p + 1) * SUB] - neighbours(wr, x)
                ii = z[(PLANES + p) * SUB : (PLANES + p + 1) * SUB] - neighbours(wi, x)
                mr, mi = mur[x], mui[x]
                vr = (1.0 - OMEGA) * (center(wr, x) - center(ur, x)) - OMEGA * (mr * ir - mi * ii)
                vi = (1.0 - OMEGA) * (center(wi, x) - center(ui, x)) - OMEGA * (mr * ii + mi * ir)
                v3r[x] = vr
                v3i[x] = vi
                qr[x + 1, FIRST : FIRST + SUB] = mr * vr + mi * vi
                qi[x + 1, FIRST : FIRST + SUB] = mr * vi - mi * vr
                gr[x] = vr * ir + vi * ii
                gi[x] = vi * ir - vr * ii
            return carry

        lax.fori_loop(0, SUB // PLANES, third, 0)

        row0 = bx0 * HALO - x_base
        col0 = pl.multiple_of((by0 + 1) * HALO, HALO)

        def fourth(step, carry):
            z = stencil_z(qr, qi, step * PLANES, tri[...])
            parts = []
            for p in range(PLANES):
                x = step * PLANES + p
                jr = z[p * SUB : (p + 1) * SUB] - neighbours(qr, x)
                ji = z[(PLANES + p) * SUB : (PLANES + p + 1) * SUB] - neighbours(qi, x)
                vr = (1.0 - OMEGA) * v3r[x] - OMEGA * jr
                vi = (1.0 - OMEGA) * v3i[x] - OMEGA * ji
                ir, ii = l1r[x], l1i[x]
                sr = -OMEGA * (gr[x] + (vr * ir + vi * ii))
                si = -OMEGA * (gi[x] + (vi * ir - vr * ii))
                parts.append(jnp.concatenate(split(sr) + split(si), axis=1))
            grad = jnp.dot(
                jnp.concatenate(parts, axis=0), gather[depth], preferred_element_type=jnp.float32
            )
            for p in range(PLANES):
                x = step * PLANES + p
                total[row0 + x, pl.ds(col0, SUB)] += grad[p * SUB : (p + 1) * SUB]
            return carry

        lax.fori_loop(0, SUB // PLANES, fourth, 0)
        return carry

    if group == 2:
        for fill in fills:
            fill.wait()

        def joined(x, carry):
            total[tx + x, HALO:] += strip[x]
            return carry

        lax.fori_loop(0, HALO, joined, 0)

    lax.fori_loop(0, count, subzone, 0)

    if group == 1:
        copies = [(total.at[:, HALO : 2 * HALO + ty], outs[0])]
    else:
        copies = [(total.at[HALO : HALO + tx, HALO : HALO + ty], outs[0])]
        if group == 2:
            copies.append((total.at[HALO : HALO + tx, HALO + ty : 2 * HALO + ty], outs[1]))
    started = []
    for index, (a, b) in enumerate(copies):
        started.append(pltpu.make_async_copy(a, b, out_sem.at[1 + index]))
        started[-1].start()
    for copy in started:
        copy.wait()


def run(group, info, sources, mats, tx, ty, *earlier):
    slots = info.shape[0] // 4
    f32 = jnp.float32
    total_rows = 2 * HALO if group == 1 else HALO + tx
    outs = {
        0: [(tx, ty, LANES)],
        1: [(2 * HALO, HALO + ty, LANES)],
        2: [(tx, ty, LANES), (tx, HALO, LANES)],
    }[group]
    hbm = pl.BlockSpec(memory_space=pl.ANY)
    smem = pl.BlockSpec(memory_space=pltpu.SMEM)
    vmem = pl.BlockSpec(memory_space=pltpu.VMEM)
    flat = [part for pair in sources for part in pair]
    args = [info] + flat + list(earlier) + list(mats)
    in_specs = [smem] + [hbm] * (len(args) - 1 - len(mats)) + [vmem] * len(mats)
    padded = pltpu.VMEM((SUB + 2, FIRST + SUB + 8, LANES), f32)
    plain = pltpu.VMEM((SUB, SUB, LANES), f32)
    return pl.pallas_call(
        functools.partial(work, group, slots, group, tx, ty, len(sources)),
        out_shape=[jax.ShapeDtypeStruct(shape, f32) for shape in outs],
        in_specs=in_specs,
        out_specs=[hbm] * len(outs),
        scratch_shapes=[
            pltpu.SMEM((slots,), jnp.int32),
            pltpu.VMEM((2, NF + 1, SUB, SUB, LANES), jnp.bfloat16),
            pltpu.VMEM((total_rows, 2 * HALO + ty, LANES), f32),
        ]
        + [padded] * 6
        + [plain] * 10
        + [pltpu.SemaphoreType.DMA((2, 4, 2)), pltpu.SemaphoreType.DMA((4,))]
        + ([pltpu.VMEM((HALO, HALO + ty, LANES), f32)] if group == 2 else []),
        compiler_params=pltpu.CompilerParams(vmem_limit_bytes=48 * 2**20),
        cost_estimate=pl.CostEstimate(
            flops=2 * 10**10 if group == 0 else 10**10, bytes_accessed=150 * 10**6, transcendentals=0
        ),
        name=("interior", "beyond_x", "beyond_y")[group],
    )(*args)


def shards(fields, modulus, anchors, home_count):
    tx, ty = modulus.shape[0], modulus.shape[1]
    n_x, n_y = lax.axis_size("vx"), lax.axis_size("vy")
    i, j = lax.axis_index("vx"), lax.axis_index("vy")
    both = ("vx", "vy")
    down_x = [(k + 1, k) for k in range(n_x - 1)]
    down_y = [(k + 1, k) for k in range(n_y - 1)]
    down_d = [
        ((a + 1) * n_y + b + 1, a * n_y + b) for a in range(n_x - 1) for b in range(n_y - 1)
    ]
    up_x = [(b, a) for a, b in down_x]
    up_y = [(b, a) for a, b in down_y]

    spots = anchors[0, 0]
    home = spots.shape[0]
    live = (jnp.arange(home, dtype=jnp.int32) < home_count[0, 0]).astype(jnp.int32)
    own = jnp.concatenate([spots, live[:, None]], axis=1)
    own_x = lax.ppermute(own, "vx", down_x)
    own_y, own_d = jnp.split(lax.ppermute(jnp.concatenate([own, own_x]), "vy", down_y), 2)
    def together(rows, cols):
        return jnp.concatenate([fields[:, rows, cols], modulus[None, rows, cols]], axis=0)

    low, full = slice(0, HALO), slice(None)
    beyond_x = lax.ppermute(together(low, full), "vx", down_x)
    corner = lax.ppermute(together(low, low), both, down_d)
    beyond_y = lax.ppermute(together(full, low), "vy", down_y)

    last_x, last_y = tx // HALO - 1, ty // HALO - 1

    def described(spot, from_x, from_y):
        o0, o1, o2, on = (spot[:, k] for k in range(4))
        ok = on > 0
        ok = ok & ((o0 == 0) if from_x else ((o0 > 0) | (i == 0)))
        ok = ok & ((o1 == 0) if from_y else ((o1 > 0) | (j == 0)))
        bx = jnp.full_like(o0, last_x) if from_x else o0 - 1
        by = jnp.full_like(o1, last_y) if from_y else o1 - 1
        kind = jnp.where(bx == last_x, 1, jnp.where(by == last_y, 2, 0))
        return jnp.stack([jnp.where(ok, kind, -1), bx, by, o2], axis=1)

    mine = described(own, False, False)
    everything = jnp.concatenate(
        [
            mine,
            described(own_x, True, False),
            described(own_y, False, True),
            described(own_d, True, True),
        ]
    )
    mats = constants()
    local = (fields, modulus)
    (inner,) = run(0, everything.reshape(-1), [local], mats, tx, ty)
    sources = [local, (beyond_y,), (beyond_x,), (corner,)]
    (strip,) = run(1, everything.reshape(-1), sources, mats, tx, ty, inner)
    from_below = lax.ppermute(strip[HALO:], "vx", up_x)
    owned, side = run(2, everything.reshape(-1), sources[:2], mats, tx, ty, inner, strip)
    side = side.at[:HALO].add(from_below[:, ty:])
    from_left = lax.ppermute(side, "vy", up_y)
    owned = owned.at[:HALO].add(from_below[:, :ty])
    return owned.at[:, :HALO].add(from_left)


def solution(mesh):
    return jax.shard_map(
        shards,
        mesh=mesh,
        in_specs=(
            P(None, "vx", "vy", None),
            P("vx", "vy", None),
            P("vx", "vy", None, None),
            P("vx", "vy"),
        ),
        out_specs=P("vx", "vy", None),
        check_vma=False,
    )
```

```python
import functools

import jax
import jax.numpy as jnp
import numpy as np
from jax import lax
from jax.experimental import pallas as pl
from jax.experimental.pallas import tpu as pltpu
from jax.sharding import PartitionSpec as P

NF = 4
SUB = 32
HALO = 16
OMEGA = 0.07
LANES = 128
NZ = 64
PLANES = 16
A_PLANES = 16
FIRST = 8


def constants():
    starts = (NZ - SUB) // HALO + 1
    second = 6.0 * np.eye(SUB) - np.eye(SUB, k=1) - np.eye(SUB, k=-1)
    tri = np.kron(np.eye(NF), second)
    pick = np.zeros((starts, NF, LANES, 4, LANES))
    spread = np.zeros((starts, LANES, 2, LANES))
    gather = np.zeros((starts, 2, 2, LANES, LANES))
    for s in range(starts):
        for f in range(NF):
            for z in range(SUB):
                for part in range(2):
                    source = part * NZ + s * HALO + z
                    lane = f * SUB + z
                    pick[s, f, source, part, lane] = 1.0
                    pick[s, f, source, 2 + part] = tri[lane]
                    spread[s, source, part, lane] = 1.0
                    gather[s, part, :, lane, source] = 1.0
    bf16 = jnp.bfloat16
    return (
        jnp.asarray(pick.reshape(starts, NF * LANES, 4 * LANES), bf16),
        jnp.asarray(spread.reshape(starts, LANES, 2 * LANES), bf16),
        jnp.asarray(gather.reshape(starts, 4 * LANES, LANES), bf16),
        jnp.asarray(np.concatenate([tri, tri], axis=0), bf16),
    )


def split(value):
    high = value.astype(jnp.bfloat16)
    low = (value - high.astype(jnp.float32)).astype(jnp.bfloat16)
    return high, low


def neighbours(ref, x):
    low = ref[x, FIRST : FIRST + SUB]
    high = ref[x + 2, FIRST : FIRST + SUB]
    left = ref[x + 1, FIRST - 1 : FIRST - 1 + SUB]
    right = ref[x + 1, FIRST + 1 : FIRST + 1 + SUB]
    return (low + high) + (left + right)


def center(ref, x):
    return ref[x + 1, FIRST : FIRST + SUB]


def stencil_z(real, imag, x, tri):
    rows = PLANES * SUB
    parts = []
    for ref in (real, imag):
        value = ref[pl.ds(x + 1, PLANES), FIRST : FIRST + SUB].reshape(rows, LANES)
        parts.append(jnp.concatenate(split(value), axis=1))
    return jnp.dot(
        jnp.concatenate(parts, axis=0), tri, preferred_element_type=jnp.float32
    )


def work(group, slots, kinds, tx, ty, n_sources, *refs):
    refs = list(refs)
    take = lambda count: [refs.pop(0) for _ in range(count)]
    (info,) = take(1)
    sources = [take(2)] + [take(1) for _ in range(n_sources - 1)]
    earlier = take(group)
    pick, spread, gather, tri = take(4)
    outs = take({0: 1, 1: 3, 2: 2}[group])
    (order, buf, total, ur, ui, wr, wi, qr, qi) = take(9)
    (zur, zui, l1r, l1i, v3r, v3i, gr, gi, mur, mui) = take(10)
    sems, out_sem = take(2)
    (strip,) = take(1) if group == 2 else (None,)

    x_base = tx - HALO if group == 1 else -HALO
    blocks = (tx // HALO, ty // HALO)

    if group == 2:
        fills = [
            pltpu.make_async_copy(
                earlier[0], total.at[HALO : HALO + tx, HALO : HALO + ty], out_sem.at[0]
            ),
            pltpu.make_async_copy(earlier[1], strip, out_sem.at[3]),
        ]
        for fill in fills:
            fill.start()
    for ref in (ur, ui, wr, wi, qr, qi):
        plane = jnp.zeros((FIRST + SUB + 8, LANES), jnp.float32)
        ref[0] = plane
        ref[SUB + 1] = plane

        def edge(x, carry, ref=ref):
            row = jnp.zeros((8, LANES), jnp.float32)
            ref[x, 0:FIRST] = row
            ref[x, FIRST + SUB :] = row
            return carry

        lax.fori_loop(1, SUB + 1, edge, 0)

    def clear(x, carry):
        if group == 2:
            side = jnp.zeros((HALO, LANES), jnp.float32)
            total[x, :HALO] = side
            total[x, HALO + ty :] = side
        else:
            total[x] = jnp.zeros(total.shape[1:], jnp.float32)
        return carry

    lax.fori_loop(0, total.shape[0], clear, 0)
    if group == 2:
        total[:HALO, HALO : HALO + ty] = jnp.zeros((HALO, ty, LANES), jnp.float32)

    def listed(slot, count):
        mine = info[4 * slot] == kinds

        @pl.when(mine)
        def _():
            order[count] = slot

        return count + jnp.where(mine, 1, 0)

    count = lax.fori_loop(0, slots, listed, jnp.int32(0))

    def place(item):
        slot = order[item]
        return info[4 * slot + 1], info[4 * slot + 2], info[4 * slot + 3]

    def transfers(item, slot, starting):
        bx0, by0, _ = place(item)
        for dx in range(2):
            for dy in range(2):
                bx, by = bx0 + dx, by0 + dy
                rows = pl.ds(dx * HALO, HALO)
                cols = pl.ds(dy * HALO, HALO)
                to_f = buf.at[slot, :NF, rows, cols, :]
                to_m = buf.at[slot, NF, rows, cols, :]
                to_all = buf.at[slot, :, rows, cols, :]
                quarter = 2 * dx + dy
                outside = (bx < 0) | (by < 0)
                past_x = bx >= blocks[0]
                past_y = by >= blocks[1]
                conditions = [jnp.logical_not(past_x) & jnp.logical_not(past_y)]
                if n_sources > 1:
                    conditions.append(jnp.logical_not(past_x) & past_y)
                if n_sources > 2:
                    conditions.append(past_x & jnp.logical_not(past_y))
                    conditions.append(past_x & past_y)
                for kind, condition in enumerate(conditions):
                    @pl.when(jnp.logical_not(outside) & condition)
                    def _(kind=kind):
                        r = 0 if kind >= 2 else pl.multiple_of(bx * HALO, HALO)
                        c = 0 if kind in (1, 3) else pl.multiple_of(by * HALO, HALO)
                        box = (pl.ds(r, HALO), pl.ds(c, HALO), slice(None))
                        first = sources[kind][0].at[(slice(None),) + box]
                        if kind == 0:
                            pairs = [(first, to_f), (sources[0][1].at[box], to_m)]
                        else:
                            pairs = [(first, to_all)]
                        for which, (a, b) in enumerate(pairs):
                            copy = pltpu.make_async_copy(a, b, sems.at[slot, quarter, which])
                            if starting:
                                copy.start()
                            else:
                                copy.wait()
                if starting:
                    @pl.when(outside)
                    def _():
                        buf[slot, :, dx * HALO : dx * HALO + HALO, dy * HALO : dy * HALO + HALO, :] = jnp.zeros(
                            (NF + 1, HALO, HALO, LANES), jnp.bfloat16
                        )

    @pl.when(count > 0)
    def _():
        transfers(jnp.int32(0), 0, True)

    def subzone(item, carry):
        slot = lax.rem(item, 2)

        @pl.when(item + 1 < count)
        def _():
            transfers(item + 1, 1 - slot, True)

        transfers(item, slot, False)
        bx0, by0, depth = place(item)

        def load(step, carry):
            x = step * A_PLANES
            rows = A_PLANES * SUB
            shape = (A_PLANES, SUB, LANES)
            block = jnp.concatenate(
                [buf[slot, f, pl.ds(x, A_PLANES)].reshape(rows, LANES) for f in range(NF)], axis=1
            )
            got = jnp.dot(block, pick[depth], preferred_element_type=jnp.float32)
            ur[pl.ds(x + 1, A_PLANES), FIRST : FIRST + SUB] = got[:, :LANES].reshape(shape)
            ui[pl.ds(x + 1, A_PLANES), FIRST : FIRST + SUB] = got[:, LANES : 2 * LANES].reshape(shape)
            zur[pl.ds(x, A_PLANES)] = got[:, 2 * LANES : 3 * LANES].reshape(shape)
            zui[pl.ds(x, A_PLANES)] = got[:, 3 * LANES :].reshape(shape)
            stiff = buf[slot, NF, pl.ds(x, A_PLANES)].reshape(rows, LANES)
            mu = jnp.dot(stiff, spread[depth], preferred_element_type=jnp.float32)
            mur[pl.ds(x, A_PLANES)] = mu[:, :LANES].reshape(shape)
            mui[pl.ds(x, A_PLANES)] = mu[:, LANES:].reshape(shape)
            return carry

        lax.fori_loop(0, SUB // A_PLANES, load, 0)

        def second(step, carry):
            for p in range(PLANES):
                x = step * PLANES + p
                ir = OMEGA * (zur[x] - neighbours(ur, x))
                ii = OMEGA * (zui[x] - neighbours(ui, x))
                l1r[x] = ir
                l1i[x] = ii
                mr, mi = mur[x], mui[x]
                keep = OMEGA * (2.0 - OMEGA)
                wr[x + 1, FIRST : FIRST + SUB] = keep * center(ur, x) - OMEGA * (mr * ir - mi * ii)
                wi[x + 1, FIRST : FIRST + SUB] = keep * center(ui, x) - OMEGA * (mr * ii + mi * ir)
            return carry

        lax.fori_loop(0, SUB // PLANES, second, 0)

        def third(step, carry):
            z = stencil_z(wr, wi, step * PLANES, tri[...])
            for p in range(PLANES):
                x = step * PLANES + p
                ir = z[p * SUB : (p + 1) * SUB] - neighbours(wr, x)
                ii = z[(PLANES + p) * SUB : (PLANES + p + 1) * SUB] - neighbours(wi, x)
                mr, mi = mur[x], mui[x]
                vr = (1.0 - OMEGA) * (center(wr, x) - center(ur, x)) - OMEGA * (mr * ir - mi * ii)
                vi = (1.0 - OMEGA) * (center(wi, x) - center(ui, x)) - OMEGA * (mr * ii + mi * ir)
                v3r[x] = vr
                v3i[x] = vi
                qr[x + 1, FIRST : FIRST + SUB] = mr * vr + mi * vi
                qi[x + 1, FIRST : FIRST + SUB] = mr * vi - mi * vr
                gr[x] = vr * ir + vi * ii
                gi[x] = vi * ir - vr * ii
            return carry

        lax.fori_loop(0, SUB // PLANES, third, 0)

        row0 = bx0 * HALO - x_base
        col0 = pl.multiple_of((by0 + 1) * HALO, HALO)

        def fourth(step, carry):
            z = stencil_z(qr, qi, step * PLANES, tri[...])
            parts = []
            for p in range(PLANES):
                x = step * PLANES + p
                jr = z[p * SUB : (p + 1) * SUB] - neighbours(qr, x)
                ji = z[(PLANES + p) * SUB : (PLANES + p + 1) * SUB] - neighbours(qi, x)
                vr = (1.0 - OMEGA) * v3r[x] - OMEGA * jr
                vi = (1.0 - OMEGA) * v3i[x] - OMEGA * ji
                ir, ii = l1r[x], l1i[x]
                sr = -OMEGA * (gr[x] + (vr * ir + vi * ii))
                si = -OMEGA * (gi[x] + (vi * ir - vr * ii))
                parts.append(jnp.concatenate(split(sr) + split(si), axis=1))
            grad = jnp.dot(
                jnp.concatenate(parts, axis=0), gather[depth], preferred_element_type=jnp.float32
            )
            for p in range(PLANES):
                x = step * PLANES + p
                total[row0 + x, pl.ds(col0, SUB)] += grad[p * SUB : (p + 1) * SUB]
            return carry

        lax.fori_loop(0, SUB // PLANES, fourth, 0)
        return carry

    if group == 2:
        for fill in fills:
            fill.wait()

        def joined(x, carry):
            total[tx + x, HALO:] += strip[x]
            return carry

        lax.fori_loop(0, HALO, joined, 0)

    lax.fori_loop(0, count, subzone, 0)

    if group == 1:
        copies = [
            (total.at[HALO:, HALO : HALO + ty], outs[1]),
            (total.at[HALO:, HALO + ty : 2 * HALO + ty], outs[2]),
            (total.at[:HALO, HALO : 2 * HALO + ty], outs[0]),
        ]
    else:
        copies = [(total.at[HALO : HALO + tx, HALO : HALO + ty], outs[0])]
        if group == 2:
            copies.append((total.at[HALO : HALO + tx, HALO + ty : 2 * HALO + ty], outs[1]))
    started = []
    for index, (a, b) in enumerate(copies):
        started.append(pltpu.make_async_copy(a, b, out_sem.at[1 + index]))
        started[-1].start()
    for copy in started:
        copy.wait()


def run(group, info, sources, mats, tx, ty, *earlier):
    slots = info.shape[0] // 4
    f32 = jnp.float32
    total_rows = 2 * HALO if group == 1 else HALO + tx
    outs = {
        0: [(tx, ty, LANES)],
        1: [(HALO, HALO + ty, LANES), (HALO, ty, LANES), (HALO, HALO, LANES)],
        2: [(tx, ty, LANES), (tx, HALO, LANES)],
    }[group]
    hbm = pl.BlockSpec(memory_space=pl.ANY)
    smem = pl.BlockSpec(memory_space=pltpu.SMEM)
    vmem = pl.BlockSpec(memory_space=pltpu.VMEM)
    flat = [part for pair in sources for part in pair]
    args = [info] + flat + list(earlier) + list(mats)
    in_specs = [smem] + [hbm] * (len(args) - 1 - len(mats)) + [vmem] * len(mats)
    padded = pltpu.VMEM((SUB + 2, FIRST + SUB + 8, LANES), f32)
    plain = pltpu.VMEM((SUB, SUB, LANES), f32)
    return pl.pallas_call(
        functools.partial(work, group, slots, group, tx, ty, len(sources)),
        out_shape=[jax.ShapeDtypeStruct(shape, f32) for shape in outs],
        in_specs=in_specs,
        out_specs=[hbm] * len(outs),
        scratch_shapes=[
            pltpu.SMEM((slots,), jnp.int32),
            pltpu.VMEM((2, NF + 1, SUB, SUB, LANES), jnp.bfloat16),
            pltpu.VMEM((total_rows, 2 * HALO + ty, LANES), f32),
        ]
        + [padded] * 6
        + [plain] * 10
        + [pltpu.SemaphoreType.DMA((2, 4, 2)), pltpu.SemaphoreType.DMA((4,))]
        + ([pltpu.VMEM((HALO, HALO + ty, LANES), f32)] if group == 2 else []),
        compiler_params=pltpu.CompilerParams(vmem_limit_bytes=48 * 2**20),
        cost_estimate=pl.CostEstimate(
            flops=2 * 10**10 if group == 0 else 10**10, bytes_accessed=150 * 10**6, transcendentals=0
        ),
        name=("interior", "beyond_x", "beyond_y")[group],
    )(*args)


def shards(fields, modulus, anchors, home_count):
    tx, ty = modulus.shape[0], modulus.shape[1]
    n_x, n_y = lax.axis_size("vx"), lax.axis_size("vy")
    i, j = lax.axis_index("vx"), lax.axis_index("vy")
    both = ("vx", "vy")
    down_x = [(k + 1, k) for k in range(n_x - 1)]
    down_y = [(k + 1, k) for k in range(n_y - 1)]
    down_d = [
        ((a + 1) * n_y + b + 1, a * n_y + b) for a in range(n_x - 1) for b in range(n_y - 1)
    ]
    up_x = [(b, a) for a, b in down_x]
    up_y = [(b, a) for a, b in down_y]
    up_d = [(b, a) for a, b in down_d]

    spots = anchors[0, 0]
    home = spots.shape[0]
    live = (jnp.arange(home, dtype=jnp.int32) < home_count[0, 0]).astype(jnp.int32)
    own = jnp.concatenate([spots, live[:, None]], axis=1)
    own_x = lax.ppermute(own, "vx", down_x)
    own_y, own_d = jnp.split(lax.ppermute(jnp.concatenate([own, own_x]), "vy", down_y), 2)
    def together(rows, cols):
        return jnp.concatenate([fields[:, rows, cols], modulus[None, rows, cols]], axis=0)

    low, full = slice(0, HALO), slice(None)
    beyond_x = lax.ppermute(together(low, full), "vx", down_x)
    corner = lax.ppermute(together(low, low), both, down_d)
    beyond_y = lax.ppermute(together(full, low), "vy", down_y)

    last_x, last_y = tx // HALO - 1, ty // HALO - 1

    def described(spot, from_x, from_y):
        o0, o1, o2, on = (spot[:, k] for k in range(4))
        ok = on > 0
        ok = ok & ((o0 == 0) if from_x else ((o0 > 0) | (i == 0)))
        ok = ok & ((o1 == 0) if from_y else ((o1 > 0) | (j == 0)))
        bx = jnp.full_like(o0, last_x) if from_x else o0 - 1
        by = jnp.full_like(o1, last_y) if from_y else o1 - 1
        kind = jnp.where(bx == last_x, 1, jnp.where(by == last_y, 2, 0))
        return jnp.stack([jnp.where(ok, kind, -1), bx, by, o2], axis=1)

    mine = described(own, False, False)
    everything = jnp.concatenate(
        [
            mine,
            described(own_x, True, False),
            described(own_y, False, True),
            described(own_d, True, True),
        ]
    )
    mats = constants()
    local = (fields, modulus)
    (inner,) = run(0, everything.reshape(-1), [local], mats, tx, ty)
    sources = [local, (beyond_y,), (beyond_x,), (corner,)]
    strip, below, edge = run(1, everything.reshape(-1), sources, mats, tx, ty, inner)
    from_below = lax.ppermute(below, "vx", up_x)
    from_corner = lax.ppermute(edge, both, up_d)
    owned, side = run(2, everything.reshape(-1), sources[:2], mats, tx, ty, inner, strip)
    from_left = lax.ppermute(side, "vy", up_y)
    from_left = from_left.at[:HALO].add(from_corner)
    owned = owned.at[:, :HALO].add(from_left)
    return owned.at[:HALO].add(from_below)


def solution(mesh):
    return jax.shard_map(
        shards,
        mesh=mesh,
        in_specs=(
            P(None, "vx", "vy", None),
            P("vx", "vy", None),
            P("vx", "vy", None, None),
            P("vx", "vy"),
        ),
        out_specs=P("vx", "vy", None),
        check_vma=False,
    )
```

```python
import functools

import jax
import jax.numpy as jnp
import numpy as np
from jax import lax
from jax.experimental import pallas as pl
from jax.experimental.pallas import tpu as pltpu
from jax.sharding import PartitionSpec as P

NF = 4
SUB = 32
HALO = 16
OMEGA = 0.07
LANES = 128
NZ = 64
PLANES = 32
A_PLANES = 16
FIRST = 8


def constants():
    starts = (NZ - SUB) // HALO + 1
    second = 6.0 * np.eye(SUB) - np.eye(SUB, k=1) - np.eye(SUB, k=-1)
    tri = np.kron(np.eye(NF), second)
    pick = np.zeros((starts, NF, LANES, 4, LANES))
    spread = np.zeros((starts, LANES, 2, LANES))
    gather = np.zeros((starts, 2, 2, LANES, LANES))
    for s in range(starts):
        for f in range(NF):
            for z in range(SUB):
                for part in range(2):
                    source = part * NZ + s * HALO + z
                    lane = f * SUB + z
                    pick[s, f, source, part, lane] = 1.0
                    pick[s, f, source, 2 + part] = tri[lane]
                    spread[s, source, part, lane] = 1.0
                    gather[s, part, :, lane, source] = 1.0
    bf16 = jnp.bfloat16
    return (
        jnp.asarray(pick.reshape(starts, NF * LANES, 4 * LANES), bf16),
        jnp.asarray(spread.reshape(starts, LANES, 2 * LANES), bf16),
        jnp.asarray(gather.reshape(starts, 4 * LANES, LANES), bf16),
        jnp.asarray(np.concatenate([tri, tri], axis=0), bf16),
    )


def split(value):
    high = value.astype(jnp.bfloat16)
    low = (value - high.astype(jnp.float32)).astype(jnp.bfloat16)
    return high, low


def neighbours(ref, x):
    low = ref[x, FIRST : FIRST + SUB]
    high = ref[x + 2, FIRST : FIRST + SUB]
    left = ref[x + 1, FIRST - 1 : FIRST - 1 + SUB]
    right = ref[x + 1, FIRST + 1 : FIRST + 1 + SUB]
    return (low + high) + (left + right)


def center(ref, x):
    return ref[x + 1, FIRST : FIRST + SUB]


def stencil_z(real, imag, x, tri):
    rows = PLANES * SUB
    parts = []
    for ref in (real, imag):
        value = ref[pl.ds(x + 1, PLANES), FIRST : FIRST + SUB].reshape(rows, LANES)
        parts.append(jnp.concatenate(split(value), axis=1))
    return jnp.dot(
        jnp.concatenate(parts, axis=0), tri, preferred_element_type=jnp.float32
    )


def work(group, slots, kinds, tx, ty, n_sources, *refs):
    refs = list(refs)
    take = lambda count: [refs.pop(0) for _ in range(count)]
    (info,) = take(1)
    sources = [take(2)] + [take(1) for _ in range(n_sources - 1)]
    earlier = take(group)
    pick, spread, gather, tri = take(4)
    outs = take({0: 1, 1: 3, 2: 2}[group])
    (order, buf, total, ur, ui, wr, wi, qr, qi) = take(9)
    (zur, zui, l1r, l1i, v3r, v3i, gr, gi, mur, mui) = take(10)
    sems, out_sem = take(2)
    (strip,) = take(1) if group == 2 else (None,)

    x_base = tx - HALO if group == 1 else -HALO
    blocks = (tx // HALO, ty // HALO)

    if group == 2:
        fills = [
            pltpu.make_async_copy(
                earlier[0], total.at[HALO : HALO + tx, HALO : HALO + ty], out_sem.at[0]
            ),
            pltpu.make_async_copy(earlier[1], strip, out_sem.at[3]),
        ]
        for fill in fills:
            fill.start()
    for ref in (ur, ui, wr, wi, qr, qi):
        plane = jnp.zeros((FIRST + SUB + 8, LANES), jnp.float32)
        ref[0] = plane
        ref[SUB + 1] = plane

        def edge(x, carry, ref=ref):
            row = jnp.zeros((8, LANES), jnp.float32)
            ref[x, 0:FIRST] = row
            ref[x, FIRST + SUB :] = row
            return carry

        lax.fori_loop(1, SUB + 1, edge, 0)

    def clear(x, carry):
        if group == 2:
            side = jnp.zeros((HALO, LANES), jnp.float32)
            total[x, :HALO] = side
            total[x, HALO + ty :] = side
        else:
            total[x] = jnp.zeros(total.shape[1:], jnp.float32)
        return carry

    lax.fori_loop(0, total.shape[0], clear, 0)
    if group == 2:
        total[:HALO, HALO : HALO + ty] = jnp.zeros((HALO, ty, LANES), jnp.float32)

    def listed(slot, count):
        mine = info[4 * slot] == kinds

        @pl.when(mine)
        def _():
            order[count] = slot

        return count + jnp.where(mine, 1, 0)

    count = lax.fori_loop(0, slots, listed, jnp.int32(0))

    def place(item):
        slot = order[item]
        return info[4 * slot + 1], info[4 * slot + 2], info[4 * slot + 3]

    def transfers(item, slot, starting):
        bx0, by0, _ = place(item)
        for dx in range(2):
            for dy in range(2):
                bx, by = bx0 + dx, by0 + dy
                rows = pl.ds(dx * HALO, HALO)
                cols = pl.ds(dy * HALO, HALO)
                to_f = buf.at[slot, :NF, rows, cols, :]
                to_m = buf.at[slot, NF, rows, cols, :]
                to_all = buf.at[slot, :, rows, cols, :]
                quarter = 2 * dx + dy
                outside = (bx < 0) | (by < 0)
                past_x = bx >= blocks[0]
                past_y = by >= blocks[1]
                conditions = [jnp.logical_not(past_x) & jnp.logical_not(past_y)]
                if n_sources > 1:
                    conditions.append(jnp.logical_not(past_x) & past_y)
                if n_sources > 2:
                    conditions.append(past_x & jnp.logical_not(past_y))
                    conditions.append(past_x & past_y)
                for kind, condition in enumerate(conditions):
                    @pl.when(jnp.logical_not(outside) & condition)
                    def _(kind=kind):
                        r = 0 if kind >= 2 else pl.multiple_of(bx * HALO, HALO)
                        c = 0 if kind in (1, 3) else pl.multiple_of(by * HALO, HALO)
                        box = (pl.ds(r, HALO), pl.ds(c, HALO), slice(None))
                        first = sources[kind][0].at[(slice(None),) + box]
                        if kind == 0:
                            pairs = [(first, to_f), (sources[0][1].at[box], to_m)]
                        else:
                            pairs = [(first, to_all)]
                        for which, (a, b) in enumerate(pairs):
                            copy = pltpu.make_async_copy(a, b, sems.at[slot, quarter, which])
                            if starting:
                                copy.start()
                            else:
                                copy.wait()
                if starting:
                    @pl.when(outside)
                    def _():
                        buf[slot, :, dx * HALO : dx * HALO + HALO, dy * HALO : dy * HALO + HALO, :] = jnp.zeros(
                            (NF + 1, HALO, HALO, LANES), jnp.bfloat16
                        )

    @pl.when(count > 0)
    def _():
        transfers(jnp.int32(0), 0, True)

    def subzone(item, carry):
        slot = lax.rem(item, 2)

        @pl.when(item + 1 < count)
        def _():
            transfers(item + 1, 1 - slot, True)

        transfers(item, slot, False)
        bx0, by0, depth = place(item)

        def load(step, carry):
            x = step * A_PLANES
            rows = A_PLANES * SUB
            shape = (A_PLANES, SUB, LANES)
            block = jnp.concatenate(
                [buf[slot, f, pl.ds(x, A_PLANES)].reshape(rows, LANES) for f in range(NF)], axis=1
            )
            got = jnp.dot(block, pick[depth], preferred_element_type=jnp.float32)
            ur[pl.ds(x + 1, A_PLANES), FIRST : FIRST + SUB] = got[:, :LANES].reshape(shape)
            ui[pl.ds(x + 1, A_PLANES), FIRST : FIRST + SUB] = got[:, LANES : 2 * LANES].reshape(shape)
            zur[pl.ds(x, A_PLANES)] = got[:, 2 * LANES : 3 * LANES].reshape(shape)
            zui[pl.ds(x, A_PLANES)] = got[:, 3 * LANES :].reshape(shape)
            stiff = buf[slot, NF, pl.ds(x, A_PLANES)].reshape(rows, LANES)
            mu = jnp.dot(stiff, spread[depth], preferred_element_type=jnp.float32)
            mur[pl.ds(x, A_PLANES)] = mu[:, :LANES].reshape(shape)
            mui[pl.ds(x, A_PLANES)] = mu[:, LANES:].reshape(shape)
            return carry

        lax.fori_loop(0, SUB // A_PLANES, load, 0)

        def second(step, carry):
            for p in range(PLANES):
                x = step * PLANES + p
                ir = OMEGA * (zur[x] - neighbours(ur, x))
                ii = OMEGA * (zui[x] - neighbours(ui, x))
                l1r[x] = ir
                l1i[x] = ii
                mr, mi = mur[x], mui[x]
                keep = OMEGA * (2.0 - OMEGA)
                wr[x + 1, FIRST : FIRST + SUB] = keep * center(ur, x) - OMEGA * (mr * ir - mi * ii)
                wi[x + 1, FIRST : FIRST + SUB] = keep * center(ui, x) - OMEGA * (mr * ii + mi * ir)
            return carry

        lax.fori_loop(0, SUB // PLANES, second, 0)

        def third(step, carry):
            z = stencil_z(wr, wi, step * PLANES, tri[...])
            for p in range(PLANES):
                x = step * PLANES + p
                ir = z[p * SUB : (p + 1) * SUB] - neighbours(wr, x)
                ii = z[(PLANES + p) * SUB : (PLANES + p + 1) * SUB] - neighbours(wi, x)
                mr, mi = mur[x], mui[x]
                vr = (1.0 - OMEGA) * (center(wr, x) - center(ur, x)) - OMEGA * (mr * ir - mi * ii)
                vi = (1.0 - OMEGA) * (center(wi, x) - center(ui, x)) - OMEGA * (mr * ii + mi * ir)
                v3r[x] = vr
                v3i[x] = vi
                qr[x + 1, FIRST : FIRST + SUB] = mr * vr + mi * vi
                qi[x + 1, FIRST : FIRST + SUB] = mr * vi - mi * vr
                gr[x] = vr * ir + vi * ii
                gi[x] = vi * ir - vr * ii
            return carry

        lax.fori_loop(0, SUB // PLANES, third, 0)

        row0 = bx0 * HALO - x_base
        col0 = pl.multiple_of((by0 + 1) * HALO, HALO)

        def fourth(step, carry):
            z = stencil_z(qr, qi, step * PLANES, tri[...])
            parts = []
            for p in range(PLANES):
                x = step * PLANES + p
                jr = z[p * SUB : (p + 1) * SUB] - neighbours(qr, x)
                ji = z[(PLANES + p) * SUB : (PLANES + p + 1) * SUB] - neighbours(qi, x)
                vr = (1.0 - OMEGA) * v3r[x] - OMEGA * jr
                vi = (1.0 - OMEGA) * v3i[x] - OMEGA * ji
                ir, ii = l1r[x], l1i[x]
                sr = -OMEGA * (gr[x] + (vr * ir + vi * ii))
                si = -OMEGA * (gi[x] + (vi * ir - vr * ii))
                parts.append(jnp.concatenate(split(sr) + split(si), axis=1))
            grad = jnp.dot(
                jnp.concatenate(parts, axis=0), gather[depth], preferred_element_type=jnp.float32
            )
            for p in range(PLANES):
                x = step * PLANES + p
                total[row0 + x, pl.ds(col0, SUB)] += grad[p * SUB : (p + 1) * SUB]
            return carry

        lax.fori_loop(0, SUB // PLANES, fourth, 0)
        return carry

    if group == 2:
        for fill in fills:
            fill.wait()

        def joined(x, carry):
            total[tx + x, HALO:] += strip[x]
            return carry

        lax.fori_loop(0, HALO, joined, 0)

    lax.fori_loop(0, count, subzone, 0)

    if group == 1:
        copies = [
            (total.at[HALO:, HALO : HALO + ty], outs[1]),
            (total.at[HALO:, HALO + ty : 2 * HALO + ty], outs[2]),
            (total.at[:HALO, HALO : 2 * HALO + ty], outs[0]),
        ]
    else:
        copies = [(total.at[HALO : HALO + tx, HALO : HALO + ty], outs[0])]
        if group == 2:
            copies.append((total.at[HALO : HALO + tx, HALO + ty : 2 * HALO + ty], outs[1]))
    started = []
    for index, (a, b) in enumerate(copies):
        started.append(pltpu.make_async_copy(a, b, out_sem.at[1 + index]))
        started[-1].start()
    for copy in started:
        copy.wait()


def run(group, info, sources, mats, tx, ty, *earlier):
    slots = info.shape[0] // 4
    f32 = jnp.float32
    total_rows = 2 * HALO if group == 1 else HALO + tx
    outs = {
        0: [(tx, ty, LANES)],
        1: [(HALO, HALO + ty, LANES), (HALO, ty, LANES), (HALO, HALO, LANES)],
        2: [(tx, ty, LANES), (tx, HALO, LANES)],
    }[group]
    hbm = pl.BlockSpec(memory_space=pl.ANY)
    smem = pl.BlockSpec(memory_space=pltpu.SMEM)
    vmem = pl.BlockSpec(memory_space=pltpu.VMEM)
    flat = [part for pair in sources for part in pair]
    args = [info] + flat + list(earlier) + list(mats)
    in_specs = [smem] + [hbm] * (len(args) - 1 - len(mats)) + [vmem] * len(mats)
    padded = pltpu.VMEM((SUB + 2, FIRST + SUB + 8, LANES), f32)
    plain = pltpu.VMEM((SUB, SUB, LANES), f32)
    return pl.pallas_call(
        functools.partial(work, group, slots, group, tx, ty, len(sources)),
        out_shape=[jax.ShapeDtypeStruct(shape, f32) for shape in outs],
        in_specs=in_specs,
        out_specs=[hbm] * len(outs),
        scratch_shapes=[
            pltpu.SMEM((slots,), jnp.int32),
            pltpu.VMEM((2, NF + 1, SUB, SUB, LANES), jnp.bfloat16),
            pltpu.VMEM((total_rows, 2 * HALO + ty, LANES), f32),
        ]
        + [padded] * 6
        + [plain] * 10
        + [pltpu.SemaphoreType.DMA((2, 4, 2)), pltpu.SemaphoreType.DMA((4,))]
        + ([pltpu.VMEM((HALO, HALO + ty, LANES), f32)] if group == 2 else []),
        compiler_params=pltpu.CompilerParams(vmem_limit_bytes=48 * 2**20),
        cost_estimate=pl.CostEstimate(
            flops=2 * 10**10 if group == 0 else 10**10, bytes_accessed=150 * 10**6, transcendentals=0
        ),
        name=("interior", "beyond_x", "beyond_y")[group],
    )(*args)


def shards(fields, modulus, anchors, home_count):
    tx, ty = modulus.shape[0], modulus.shape[1]
    n_x, n_y = lax.axis_size("vx"), lax.axis_size("vy")
    i, j = lax.axis_index("vx"), lax.axis_index("vy")
    both = ("vx", "vy")
    down_x = [(k + 1, k) for k in range(n_x - 1)]
    down_y = [(k + 1, k) for k in range(n_y - 1)]
    down_d = [
        ((a + 1) * n_y + b + 1, a * n_y + b) for a in range(n_x - 1) for b in range(n_y - 1)
    ]
    up_x = [(b, a) for a, b in down_x]
    up_y = [(b, a) for a, b in down_y]
    up_d = [(b, a) for a, b in down_d]

    spots = anchors[0, 0]
    home = spots.shape[0]
    live = (jnp.arange(home, dtype=jnp.int32) < home_count[0, 0]).astype(jnp.int32)
    own = jnp.concatenate([spots, live[:, None]], axis=1)
    own_x = lax.ppermute(own, "vx", down_x)
    own_y, own_d = jnp.split(lax.ppermute(jnp.concatenate([own, own_x]), "vy", down_y), 2)
    def together(rows, cols):
        return jnp.concatenate([fields[:, rows, cols], modulus[None, rows, cols]], axis=0)

    low, full = slice(0, HALO), slice(None)
    beyond_x = lax.ppermute(together(low, full), "vx", down_x)
    corner = lax.ppermute(together(low, low), both, down_d)
    beyond_y = lax.ppermute(together(full, low), "vy", down_y)

    last_x, last_y = tx // HALO - 1, ty // HALO - 1

    def described(spot, from_x, from_y):
        o0, o1, o2, on = (spot[:, k] for k in range(4))
        ok = on > 0
        ok = ok & ((o0 == 0) if from_x else ((o0 > 0) | (i == 0)))
        ok = ok & ((o1 == 0) if from_y else ((o1 > 0) | (j == 0)))
        bx = jnp.full_like(o0, last_x) if from_x else o0 - 1
        by = jnp.full_like(o1, last_y) if from_y else o1 - 1
        kind = jnp.where(bx == last_x, 1, jnp.where(by == last_y, 2, 0))
        return jnp.stack([jnp.where(ok, kind, -1), bx, by, o2], axis=1)

    mine = described(own, False, False)
    everything = jnp.concatenate(
        [
            mine,
            described(own_x, True, False),
            described(own_y, False, True),
            described(own_d, True, True),
        ]
    )
    mats = constants()
    local = (fields, modulus)
    (inner,) = run(0, everything.reshape(-1), [local], mats, tx, ty)
    sources = [local, (beyond_y,), (beyond_x,), (corner,)]
    strip, below, edge = run(1, everything.reshape(-1), sources, mats, tx, ty, inner)
    from_below = lax.ppermute(below, "vx", up_x)
    from_corner = lax.ppermute(edge, both, up_d)
    owned, side = run(2, everything.reshape(-1), sources[:2], mats, tx, ty, inner, strip)
    from_left = lax.ppermute(side, "vy", up_y)
    from_left = from_left.at[:HALO].add(from_corner)
    owned = owned.at[:, :HALO].add(from_left)
    return owned.at[:HALO].add(from_below)


def solution(mesh):
    return jax.shard_map(
        shards,
        mesh=mesh,
        in_specs=(
            P(None, "vx", "vy", None),
            P("vx", "vy", None),
            P("vx", "vy", None, None),
            P("vx", "vy"),
        ),
        out_specs=P("vx", "vy", None),
        check_vma=False,
    )
```
